128 devices in a mesh: seq: 32 (over z, x, core), ch: 4 (over y).
Axes of the slice: x: 4, y: 4, z: 4, core: 2. Of those that a mesh axis runs over, the one named last changes fastest.
Arguments:
- tokens: bfloat16 [16384, 2048], P('seq', 'ch'), may hold values from -6 to 6
- w_in: bfloat16 [2048, 3, 2048], P(None, None, 'ch'), may hold values from -0.125 to 0.125
- short_filter: float32 [3, 3, 2048], P(None, None, 'ch'), may hold values from -3 to 3
- decay: float32 [16, 2048], P(None, 'ch'), may hold values from 6.1035156e-05 to 0.05
- residue: float32 [16, 2048], P(None, 'ch'), may hold values from -1.5 to 1.5
- skip: float32 [2048], P('ch'), may hold values from 0.5 to 1.5
- w_out: bfloat16 [2048, 2048], P(None, 'ch'), may hold values from -0.125 to 0.125
Outputs:
- mixed: bfloat16 [16384, 2048], P('seq', 'ch')
The draws below stay inside these ranges and needn't reach their ends.
All inputs are finite; a program needn't handle non-finite values.
Results may differ from the reference program's by a relative error of at most 0.009.
Values may be sent and summed in bfloat16 or wider, within the bound.
No kernel may reach another device: no remote copies, remote signals or barrier semaphores. Data moves between devices by JAX's collectives and lax.ppermute only.
A program may use at most 192 MiB of HBM per device.

```python
import math
import jax
import jax.numpy as jnp

D = 2048
MODES = 16
SHORT = 3
LENGTH = 16384


def level_of(own_key, extent, pieces, smallest, high):
    def one(position, parts):
        steps = jax.random.uniform(jax.random.fold_in(jax.random.fold_in(own_key, 6), position), (parts,), jnp.float32, smallest / len(pieces), high / len(pieces))
        return jnp.repeat(jnp.exp(steps), extent[position] // parts).reshape((-1,) + (1,) * (len(extent) - position - 1))

    level = one(*pieces[0])
    for cut in pieces[1:]:
        level = level * one(*cut)
    return level


def centred(key, extent, width, reach, cuts=(), kind=jnp.bfloat16):
    result = width * jax.random.normal(key, extent, jnp.float32)
    if cuts:
        result = result * level_of(key, extent, cuts, -0.22, 0.18)
    return jnp.clip(result, -reach, reach).astype(kind)


def setup_inputs(seed: int = 0) -> dict:
    arg_keys = jax.random.split(jax.random.key(seed), 8)
    return {
        "tokens": centred(arg_keys[0], (LENGTH, D), 1.0, 6.0, ((0, 32), (1, 4))),
        "w_in": centred(arg_keys[1], (D, 3, D), D ** -0.5, 0.125, ((2, 4),)),
        "short_filter": centred(arg_keys[2], (3, SHORT, D), 0.6, 3.0, ((2, 4),), jnp.float32),
        "decay": jnp.clip(jnp.exp(math.log(0.05) - 6.7083283 * jax.random.uniform(arg_keys[3], (MODES, D), jnp.float32) ** level_of(arg_keys[3], (MODES, D), ((1, 4),), -0.2, 0.2)), 6.103515625e-05, 0.05),
        "residue": centred(arg_keys[4], (MODES, D), MODES ** -0.5, 1.5, ((1, 4),), jnp.float32),
        "skip": jnp.clip(0.5 + 1.0 * jax.random.uniform(arg_keys[5], (D,), jnp.float32) ** level_of(arg_keys[5], (D,), ((0, 4),), -0.2, 0.2), 0.5, 1.5),
        "w_out": centred(arg_keys[6], (D, D), D ** -0.5, 0.125, ((1, 4),)),
    }


def reference(tokens, w_in, short_filter, decay, residue, skip, w_out):
    proj = jnp.dot(tokens, w_in.reshape(D, 3 * D), preferred_element_type=jnp.float32).astype(jnp.bfloat16)
    proj = proj.astype(jnp.float32).reshape(LENGTH, 3, D)
    padded = jnp.concatenate([jnp.zeros((SHORT - 1, 3, D), jnp.float32), proj], 0)
    filtered = jnp.zeros((LENGTH, 3, D), jnp.float32)
    for lag in range(SHORT):
        filtered = filtered + short_filter[:, lag, :] * padded[SHORT - 1 - lag:SHORT - 1 - lag + LENGTH]
    query = filtered[:, 0]
    signal = filtered[:, 1] * filtered[:, 2]
    times = jnp.arange(LENGTH, dtype=jnp.float32)[:, None]
    response = jnp.zeros((LENGTH, D), jnp.float32)
    for mode in range(MODES):
        response = response + residue[mode] * jnp.sqrt(decay[mode]) * jnp.exp(-decay[mode] * times)
    spectrum = jnp.fft.rfft(signal, n=2 * LENGTH, axis=0) * jnp.fft.rfft(response, n=2 * LENGTH, axis=0)
    conv = jnp.fft.irfft(spectrum, n=2 * LENGTH, axis=0)[:LENGTH]
    gated = (query * (conv + skip * signal)).astype(jnp.bfloat16)
    return jnp.dot(gated, w_out, preferred_element_type=jnp.float32).astype(jnp.bfloat16)
```

```python
from functools import partial

import jax
import jax.numpy as jnp
from jax import lax
from jax.experimental import pallas as pl
from jax.experimental.pallas import tpu as pltpu
from jax.sharding import PartitionSpec as P

LANES = 128
SUB = 8
F32 = jnp.float32
BF16 = jnp.bfloat16
MIB = 1 << 20


def vmem():
    return pl.BlockSpec(memory_space=pltpu.VMEM)


def smem():
    return pl.BlockSpec(memory_space=pltpu.SMEM)


def near(x):
    return pltpu.with_memory_space_constraint(x, pltpu.VMEM)


def params(mib=24):
    return pltpu.CompilerParams(vmem_limit_bytes=mib * MIB)


def cost(flops, nbytes, exps=0):
    return pl.CostEstimate(flops=flops, bytes_accessed=nbytes, transcendentals=exps)


def turn(block, distance):
    count = lax.axis_size("ch")
    return lax.ppermute(block, "ch", [(i, (i + distance) % count) for i in range(count)])


def ring(low, high):
    low_left, low_right = turn(low, 1), turn(low, -1)
    high_left, high_right = turn(high, 1), turn(high, -1)
    low_far = turn(low_left, 1)
    high_far = turn(high_right, -1)
    return (low, low_left, low_right, low_far), (high, high_left, high_right, high_far)


def project_kernel(me_ref, own, left, right, far, w_ref, out_ref):
    me = me_ref[0]
    depth = own.shape[1]
    for stream in range(w_ref.shape[0]):
        total = jnp.zeros((own.shape[0], w_ref.shape[2]), F32)
        for block, step in ((own, 0), (left, 3), (right, 1), (far, 2)):
            start = pl.multiple_of(lax.rem(me + step, 4) * depth, depth)
            total += jnp.dot(
                block[...], w_ref[stream, pl.ds(start, depth), :], preferred_element_type=F32
            )
        out_ref[stream] = total.astype(BF16)


def project(me, blocks, weights):
    rows = blocks[0].shape[0]
    streams, depth, cols = weights.shape
    return pl.pallas_call(
        project_kernel,
        out_shape=pltpu.VMEM((streams, rows, cols), BF16),
        in_specs=[smem()] + [vmem()] * 5,
        out_specs=vmem(),
        compiler_params=params(),
        cost_estimate=cost(2 * rows * depth * streams * cols, 4 * MIB),
        name="project",
    )(me, *[near(b) for b in blocks], near(weights))


def widen(ext, low, high, halo, stream, slot):
    half = low.shape[1]
    ext[slot, 0:SUB, :] = halo[stream, 8:16, :].astype(F32)

    @pl.loop(0, half // 16)
    def _(i):
        at = pl.multiple_of(i * 16, 16)
        ext[slot, pl.ds(at + SUB, 16), :] = low[stream, pl.ds(at, 16), :].astype(F32)
        ext[slot, pl.ds(at + SUB + half, 16), :] = high[stream, pl.ds(at, 16), :].astype(F32)


def filtered(ext, slot, taps, stream, at, size, lanes):
    total = taps[stream, 0:1, lanes] * ext[slot, pl.ds(at + SUB, size), lanes]
    for lag in range(1, 3):
        total += taps[stream, lag : lag + 1, lanes] * ext[slot, pl.ds(at + SUB - lag, size), lanes]
    return total


def state_kernel(low, high, halo, taps, decay, sig_ref, sub_ref, end_ref, ext):
    tiles, rows, _ = sig_ref.shape
    modes = decay.shape[0]
    steps = rows // SUB
    widen(ext, low, high, halo, 1, 0)
    widen(ext, low, high, halo, 2, 1)
    for tile in range(tiles):
        lanes = slice(tile * LANES, (tile + 1) * LANES)

        for at in range(0, rows, 64):
            sig_ref[tile, pl.ds(at, 64), :] = filtered(
                ext, 0, taps, 1, at, 64, lanes
            ) * filtered(ext, 1, taps, 2, at, 64, lanes)

        rates = [jnp.broadcast_to(decay[m : m + 1, lanes], (SUB, LANES)) for m in range(modes)]
        fade = [jnp.exp(-r) for r in rates]

        def step(i, held):
            now = sig_ref[tile, pl.ds(i, SUB, stride=steps), :]
            return tuple(f * h + now for f, h in zip(fade, held))

        zero = tuple(jnp.zeros((SUB, LANES), F32) for _ in range(modes))
        held = lax.fori_loop(0, steps, step, zero, unroll=8)
        later = (SUB - 1 - lax.broadcasted_iota(jnp.int32, (SUB, LANES), 0)).astype(F32) * steps
        for m in range(modes):
            sub_ref[m, :, lanes] = held[m]
            end_ref[m : m + 1, lanes] = jnp.sum(
                held[m] * jnp.exp(-rates[m] * later), axis=0, keepdims=True
            )


def local_kernel(low, high, halo, taps, decay, residue, skip, sig, sub, query_ref, part_ref, ext):
    tiles, rows, _ = sig.shape
    modes = decay.shape[0]
    steps = rows // SUB
    widen(ext, low, high, halo, 0, 0)
    place = lax.broadcasted_iota(jnp.int32, (SUB, LANES), 0)
    for tile in range(tiles):
        lanes = slice(tile * LANES, (tile + 1) * LANES)

        for at in range(0, rows, 64):
            query_ref[tile, pl.ds(at, 64), :] = filtered(ext, 0, taps, 0, at, 64, lanes)

        rates = [jnp.broadcast_to(decay[m : m + 1, lanes], (SUB, LANES)) for m in range(modes)]
        fade = [jnp.exp(-r) for r in rates]
        gain = [residue[m : m + 1, lanes] * jnp.sqrt(r) for m, r in enumerate(rates)]
        direct = jnp.broadcast_to(skip[0:1, lanes], (SUB, LANES))
        start = []
        for m in range(modes):
            run = jnp.where(place >= 1, pltpu.roll(sub[m, :, lanes], 1, 0), 0.0)
            for shift in (1, 2, 4):
                before = jnp.where(place >= shift, pltpu.roll(run, shift, 0), 0.0)
                run = run + jnp.exp(-rates[m] * float(steps * shift)) * before
            start.append(run)

        def step(i, held):
            now = sig[tile, pl.ds(i, SUB, stride=steps), :]
            held = tuple(f * h + now for f, h in zip(fade, held))
            terms = [g * h for g, h in zip(gain, held)] + [direct * now]
            while len(terms) > 1:
                terms = [sum(terms[j : j + 2]) for j in range(0, len(terms), 2)]
            part_ref[tile, pl.ds(i, SUB, stride=steps), :] = terms[0]
            return held

        lax.fori_loop(0, steps, step, tuple(start), unroll=4)


def gate_kernel(query, part, state, decay, residue, low_ref, high_ref):
    tiles, rows, _ = query.shape
    modes = decay.shape[0]
    half = rows // 2
    ahead = 1.0 + lax.broadcasted_iota(jnp.int32, (SUB, LANES), 0).astype(F32)
    for tile in range(tiles):
        lanes = slice(tile * LANES, (tile + 1) * LANES)
        rates = [jnp.broadcast_to(decay[m : m + 1, lanes], (SUB, LANES)) for m in range(modes)]
        fade = [jnp.exp(-float(SUB) * r) for r in rates]
        first = tuple(
            residue[m : m + 1, lanes] * state[m : m + 1, lanes] * jnp.sqrt(r) * jnp.exp(-r * ahead)
            for m, r in enumerate(rates)
        )

        def piece(at, held):
            terms = list(held)
            while len(terms) > 1:
                terms = [sum(terms[j : j + 2]) for j in range(0, len(terms), 2)]
            value = query[tile, pl.ds(at, SUB), :] * (part[tile, pl.ds(at, SUB), :] + terms[0])
            return value, tuple(f * h for f, h in zip(fade, held))

        def step(out_ref, base, i, held):
            at = pl.multiple_of(i * 16, 16)
            one, held = piece(at + base, held)
            two, held = piece(at + base + SUB, held)
            out_ref[pl.ds(at, 16), lanes] = jnp.concatenate([one, two], 0).astype(BF16)
            return held

        held = lax.fori_loop(0, half // 16, partial(step, low_ref, 0), first, unroll=2)
        lax.fori_loop(0, half // 16, partial(step, high_ref, half), held, unroll=2)


def mix_kernel(me_ref, own, left, right, far, w_ref, *rest):
    out_ref = rest[-1]
    me = me_ref[0]
    depth = own.shape[1]
    total = jnp.zeros(out_ref.shape, F32)
    for block, step in ((own, 0), (left, 3), (right, 1), (far, 2)):
        start = pl.multiple_of(lax.rem(me + step, 4) * depth, depth)
        total += jnp.dot(block[...], w_ref[pl.ds(start, depth), :], preferred_element_type=F32)
    out_ref[...] = total.astype(BF16)


def mix(me, blocks, weights, half, earlier):
    rows = blocks[0].shape[0]
    depth, cols = weights.shape
    aliases = {} if earlier is None else {6: 0}
    extra = () if earlier is None else (earlier,)
    return pl.pallas_call(
        mix_kernel,
        out_shape=jax.ShapeDtypeStruct((2 * rows, cols), BF16),
        grid=(1,),
        in_specs=[smem()] + [vmem()] * 5 + [pl.BlockSpec(memory_space=pl.ANY)] * len(extra),
        out_specs=pl.BlockSpec((rows, cols), lambda i: (half, 0)),
        input_output_aliases=aliases,
        compiler_params=params(),
        cost_estimate=cost(2 * rows * depth * cols, 2 * MIB),
        name="mix",
    )(me, *[near(b) for b in blocks], near(weights), *extra)


def carry_in(end, decay, rows):
    place = lax.axis_index("seq")
    devices = lax.axis_size("seq")
    state = jnp.zeros_like(end)
    span = 1
    while span < devices:
        other = lax.ppermute(end, "seq", [(i, i ^ span) for i in range(devices)])
        upper = (place // span) % 2 == 1
        gone = (rows * (place % span)).astype(F32)
        state = state + jnp.where(upper, jnp.exp(-decay * gone) * other, 0.0)
        through = jnp.exp(-decay * float(rows * span))
        end = through * jnp.where(upper, other, end) + jnp.where(upper, end, other)
        span *= 2
    return state


def shards(tokens, w_in, short_filter, decay, residue, skip, w_out):
    rows = tokens.shape[0]
    channels = skip.shape[0]
    modes = decay.shape[0]
    half = rows // 2
    me = lax.axis_index("ch").astype(jnp.int32).reshape(1)
    weights = jnp.transpose(w_in, (1, 0, 2))
    low_tok, high_tok = ring(tokens[:half], tokens[half:])
    high = project(me, high_tok, weights)
    low = project(me, low_tok, weights)
    count = lax.axis_size("seq")
    halo = lax.ppermute(high[:, half - 16 :], "seq", [(i, i + 1) for i in range(count - 1)])
    tiled = (channels // LANES, rows, LANES)
    sig, sub, end = pl.pallas_call(
        state_kernel,
        out_shape=(
            pltpu.VMEM(tiled, F32),
            pltpu.VMEM((modes, SUB, channels), F32),
            pltpu.VMEM((modes, channels), F32),
        ),
        in_specs=[vmem()] * 5,
        out_specs=(vmem(),) * 3,
        scratch_shapes=[pltpu.VMEM((2, rows + SUB, channels), F32)],
        compiler_params=params(),
        cost_estimate=cost(2 * rows * channels * modes, 4 * MIB),
        name="state",
    )(near(low), near(high), near(halo), near(short_filter), near(decay))
    query, part = pl.pallas_call(
        local_kernel,
        out_shape=(pltpu.VMEM(tiled, F32), pltpu.VMEM(tiled, F32)),
        in_specs=[vmem()] * 9,
        out_specs=(vmem(),) * 2,
        scratch_shapes=[pltpu.VMEM((1, rows + SUB, channels), F32)],
        compiler_params=params(),
        cost_estimate=cost(4 * rows * channels * modes, 6 * MIB),
        name="local",
    )(
        near(low),
        near(high),
        near(halo),
        near(short_filter),
        near(decay),
        near(residue),
        near(skip.reshape(1, channels)),
        near(sig),
        near(sub),
    )
    state = carry_in(end, decay, rows)
    gated = pl.pallas_call(
        gate_kernel,
        out_shape=(pltpu.VMEM((half, channels), BF16), pltpu.VMEM((half, channels), BF16)),
        in_specs=[vmem()] * 5,
        out_specs=(vmem(),) * 2,
        compiler_params=params(),
        cost_estimate=cost(2 * rows * channels * modes, 3 * MIB),
        name="gate",
    )(near(query), near(part), near(state), near(decay), near(residue))
    low_gate, high_gate = ring(*gated)
    out = mix(me, low_gate, w_out, 0, None)
    return mix(me, high_gate, w_out, 1, out)


def solution(mesh):
    in_specs = (
        P("seq", "ch"),
        P(None, None, "ch"),
        P(None, None, "ch"),
        P(None, "ch"),
        P(None, "ch"),
        P("ch"),
        P(None, "ch"),
    )
    return jax.shard_map(
        shards, mesh=mesh, in_specs=in_specs, out_specs=P("seq", "ch"), check_vma=False
    )
```

```python
from functools import partial

import jax
import jax.numpy as jnp
from jax import lax
from jax.experimental import pallas as pl
from jax.experimental.pallas import tpu as pltpu
from jax.sharding import PartitionSpec as P

LANES = 128
SUB = 8
F32 = jnp.float32
BF16 = jnp.bfloat16
MIB = 1 << 20


def vmem():
    return pl.BlockSpec(memory_space=pltpu.VMEM)


def near(x):
    return pltpu.with_memory_space_constraint(x, pltpu.VMEM)


def params(mib=24):
    return pltpu.CompilerParams(vmem_limit_bytes=mib * MIB)


def cost(flops, nbytes, exps=0):
    return pl.CostEstimate(flops=flops, bytes_accessed=nbytes, transcendentals=exps)


def turn(block, distance):
    count = lax.axis_size("ch")
    return lax.ppermute(block, "ch", [(i, (i + distance) % count) for i in range(count)])


def ring(low, high, work=None):
    low_left, low_right = turn(low, 1), turn(low, -1)
    high_left, high_right = turn(high, 1), turn(high, -1)
    done = None
    if work is not None:
        done = work(low, high)
        done, high_right = lax.optimization_barrier((done, high_right))
    high_far = turn(high_right, -1)
    low_far = turn(low_left, 1)
    return (low, low_left, low_right, low_far), (high, high_left, high_right, high_far), done


def source(step, depth):
    owner = lax.rem(lax.axis_index("ch") + step, 4)
    return pl.ds(pl.multiple_of(owner * depth, depth), depth)


def own_kernel(low, high, w_ref, low_ref, high_ref):
    depth = low.shape[1]
    for stream in range(w_ref.shape[0]):
        part = w_ref[stream, source(0, depth), :]
        low_ref[stream] = jnp.dot(low[...], part, preferred_element_type=F32)
        high_ref[stream] = jnp.dot(high[...], part, preferred_element_type=F32)


def near_kernel(part, left, right, w_ref, out_ref):
    depth = left.shape[1]
    for stream in range(w_ref.shape[0]):
        total = part[stream]
        for block, step in ((left, 3), (right, 1)):
            total += jnp.dot(
                block[...], w_ref[stream, source(step, depth), :], preferred_element_type=F32
            )
        out_ref[stream] = total


def high_kernel(part, left, right, far, w_ref, out_ref):
    depth = left.shape[1]
    for stream in range(w_ref.shape[0]):
        total = part[stream]
        for block, step in ((left, 3), (right, 1), (far, 2)):
            total += jnp.dot(
                block[...], w_ref[stream, source(step, depth), :], preferred_element_type=F32
            )
        out_ref[stream] = total.astype(BF16)


def filtered(ext, slot, taps, stream, at, size, lanes, width):
    total = taps[stream, 0:1, lanes] * ext[slot, pl.ds(at + SUB, size), width]
    for lag in range(1, 3):
        total += taps[stream, lag : lag + 1, lanes] * ext[slot, pl.ds(at + SUB - lag, size), width]
    return total


def tile_of(tile):
    return slice(tile * LANES, (tile + 1) * LANES)


def spread(ref, row, lanes):
    return jnp.broadcast_to(ref[row : row + 1, lanes], (SUB, LANES))


def tree(terms):
    while len(terms) > 1:
        terms = [sum(terms[j : j + 2]) for j in range(0, len(terms), 2)]
    return terms[0]


def scan_ends(sig_ref, sub_ref, end_ref, decay, tile, rows):
    lanes = tile_of(tile)
    modes = decay.shape[0]
    steps = rows // SUB
    rates = [spread(decay, m, lanes) for m in range(modes)]
    fade = [jnp.exp(-r) for r in rates]

    def step(i, held):
        now = sig_ref[tile, pl.ds(i, SUB, stride=steps), :]
        return tuple(f * h + now for f, h in zip(fade, held))

    zero = tuple(jnp.zeros((SUB, LANES), F32) for _ in range(modes))
    held = lax.fori_loop(0, steps, step, zero, unroll=8)
    later = (SUB - 1 - lax.broadcasted_iota(jnp.int32, (SUB, LANES), 0)).astype(F32) * steps
    for m in range(modes):
        sub_ref[m, :, lanes] = held[m]
        end_ref[m : m + 1, lanes] = jnp.sum(
            held[m] * jnp.exp(-rates[m] * later), axis=0, keepdims=True
        )


def late_kernel(high, taps, decay, sig_ref, sub_ref, end_ref, ext):
    tiles, rows, _ = sig_ref.shape
    ext[:, 0:SUB, :] = jnp.zeros((2, SUB, ext.shape[2]), F32)
    for slot in range(2):
        for at in range(0, rows, 64):
            ext[slot, pl.ds(at + SUB, 64), :] = high[slot + 1, pl.ds(at, 64), :].astype(F32)
    kept = lax.broadcasted_iota(jnp.int32, (64, LANES), 0) >= 2
    for tile in range(tiles):
        lanes = tile_of(tile)
        for at in range(0, rows, 64):
            value = filtered(ext, 0, taps, 1, at, 64, lanes, lanes)
            value *= filtered(ext, 1, taps, 2, at, 64, lanes, lanes)
            if at == 0:
                value = jnp.where(kept, value, 0.0)
            sig_ref[tile, pl.ds(at, 64), :] = value
        scan_ends(sig_ref, sub_ref, end_ref, decay, tile, rows)


def early_kernel(
    part, far, w_ref, high, halo, taps, decay, late_end, sig_ref, sub_ref, mid_ref, end_ref, ext
):
    tiles, rows, _ = sig_ref.shape
    rows -= SUB
    depth = far.shape[1]
    for slot in range(2):
        total = part[slot + 1] + jnp.dot(
            far[...], w_ref[slot + 1, source(2, depth), :], preferred_element_type=F32
        )
        ext[slot, pl.ds(SUB, rows), :] = total.astype(BF16).astype(F32)
        ext[slot, 0:SUB, :] = halo[slot + 1, 8:16, :].astype(F32)
        ext[slot, pl.ds(SUB + rows, SUB), :] = high[slot + 1, 0:16, :].astype(F32)[0:SUB]
    for tile in range(tiles):
        lanes = tile_of(tile)
        for at in range(0, rows + SUB, 64):
            size = min(64, rows + SUB - at)
            value = filtered(ext, 0, taps, 1, at, size, lanes, lanes)
            sig_ref[tile, pl.ds(at, size), :] = value * filtered(
                ext, 1, taps, 2, at, size, lanes, lanes
            )
        scan_ends(sig_ref, sub_ref, mid_ref, decay, tile, rows)
        rate = decay[:, lanes]
        end_ref[:, lanes] = (
            jnp.exp(-float(rows) * rate) * mid_ref[:, lanes]
            + late_end[:, lanes]
            + jnp.exp(-float(rows - 1) * rate) * sig_ref[tile, rows : rows + 1, :]
            + jnp.exp(-float(rows - 2) * rate) * sig_ref[tile, rows + 1 : rows + 2, :]
        )


def local_kernel(
    tile,
    part,
    far,
    w_ref,
    high,
    halo,
    taps,
    decay,
    residue,
    skip,
    low_sig,
    low_sub,
    mid,
    high_sig,
    high_sub,
    query_ref,
    out_ref,
    ext,
):
    lanes = tile_of(tile)
    whole = slice(0, LANES)
    modes = decay.shape[0]
    rows = high_sig.shape[1]
    steps = rows // SUB
    depth = far.shape[1]
    total = part[0, :, lanes] + jnp.dot(
        far[...], w_ref[0, source(2, depth), lanes], preferred_element_type=F32
    )
    ext[0, pl.ds(SUB, rows), :] = total.astype(BF16).astype(F32)
    ext[0, 0:SUB, :] = halo[0, 8:16, lanes].astype(F32)
    ext[0, pl.ds(SUB + rows, rows), :] = high[0, :, lanes].astype(F32)
    for at in range(0, 2 * rows, 64):
        query_ref[pl.ds(at, 64), :] = filtered(ext, 0, taps, 0, at, 64, lanes, whole)

    place = lax.broadcasted_iota(jnp.int32, (SUB, LANES), 0)
    rates = [spread(decay, m, lanes) for m in range(modes)]
    fade = [jnp.exp(-r) for r in rates]
    gain = [residue[m : m + 1, lanes] * jnp.sqrt(r) for m, r in enumerate(rates)]
    direct = spread(skip, 0, lanes)
    one = low_sig[tile, rows : rows + 1, :]
    two = low_sig[tile, rows + 1 : rows + 2, :]

    def entering(sub, first, m):
        run = jnp.where(place >= 1, pltpu.roll(sub, 1, 0), first)
        for shift in (1, 2, 4):
            before = jnp.where(place >= shift, pltpu.roll(run, shift, 0), 0.0)
            run = run + jnp.exp(-rates[m] * float(steps * shift)) * before
        return run

    def advance(held, now, at):
        held = tuple(f * h + now for f, h in zip(fade, held))
        out_ref[pl.ds(at, SUB, stride=steps), :] = tree(
            [g * h for g, h in zip(gain, held)] + [direct * now]
        )
        return held

    held = tuple(entering(low_sub[m, :, lanes], 0.0, m) for m in range(modes))
    lax.fori_loop(
        0,
        steps,
        lambda i, h: advance(h, low_sig[tile, pl.ds(i, SUB, stride=steps), :], i),
        held,
        unroll=4,
    )
    held = []
    for m in range(modes):
        sub = high_sub[m, :, lanes]
        extra = jnp.exp(-rates[m] * float(steps - 1)) * one + jnp.exp(-rates[m] * float(steps - 2)) * two
        held.append(entering(sub + jnp.where(place == 0, extra, 0.0), mid[m : m + 1, lanes], m))
    held = tuple(held)
    for i, row in ((0, one), (1, two)):
        now = high_sig[tile, pl.ds(i, SUB, stride=steps), :]
        held = advance(held, now + jnp.where(place == 0, row, 0.0), rows + i)
    lax.fori_loop(
        2,
        steps,
        lambda i, h: advance(h, high_sig[tile, pl.ds(i, SUB, stride=steps), :], rows + i),
        held,
        unroll=3,
    )


def gate_kernel(base, *refs):
    tiles = 4
    query, part = refs[:tiles], refs[tiles : 2 * tiles]
    state, decay, residue, out_ref = refs[2 * tiles :]
    modes = decay.shape[0]
    rows = out_ref.shape[0]
    ahead = float(base + 1) + lax.broadcasted_iota(jnp.int32, (SUB, LANES), 0).astype(F32)
    for tile in range(tiles):
        lanes = tile_of(tile)
        rates = [spread(decay, m, lanes) for m in range(modes)]
        fade = [jnp.exp(-float(SUB) * r) for r in rates]
        first = tuple(
            residue[m : m + 1, lanes] * state[m : m + 1, lanes] * jnp.sqrt(r) * jnp.exp(-r * ahead)
            for m, r in enumerate(rates)
        )

        def piece(at, held):
            value = query[tile][pl.ds(at + base, SUB), :] * (
                part[tile][pl.ds(at + base, SUB), :] + tree(list(held))
            )
            return value, tuple(f * h for f, h in zip(fade, held))

        def step(i, held):
            at = pl.multiple_of(i * 16, 16)
            one, held = piece(at, held)
            two, held = piece(at + SUB, held)
            out_ref[pl.ds(at, 16), lanes] = jnp.concatenate([one, two], 0).astype(BF16)
            return held

        lax.fori_loop(0, rows // 16, step, first, unroll=4)


def mix_kernel(plan, w_ref, *refs):
    blocks, rest = refs[: len(plan)], refs[len(plan) :]
    out_ref = rest[-1]
    depth = blocks[0].shape[1]
    total = None if len(rest) == 1 or rest[0].dtype != F32 else rest[0][...]
    for block, step in zip(blocks, plan):
        term = jnp.dot(block[...], w_ref[source(step, depth), :], preferred_element_type=F32)
        total = term if total is None else total + term
    out_ref[...] = total.astype(out_ref.dtype)


def mix(weights, blocks, plan):
    rows, depth = blocks[0].shape
    cols = weights.shape[1]
    return pl.pallas_call(
        partial(mix_kernel, plan),
        out_shape=pltpu.VMEM((rows, cols), F32),
        in_specs=[vmem()] * (1 + len(plan)),
        out_specs=vmem(),
        compiler_params=params(),
        cost_estimate=cost(2 * rows * depth * cols * len(plan), 2 * MIB),
        name="mix_part",
    )(weights, *[near(b) for b in blocks])


def mix_out(weights, blocks, plan, half, partial_sum, earlier):
    rows, depth = blocks[0].shape
    cols = weights.shape[1]
    args = [weights, *[near(b) for b in blocks]]
    specs = [vmem()] * (1 + len(plan))
    if partial_sum is not None:
        args.append(partial_sum)
        specs.append(vmem())
    aliases = {}
    if earlier is not None:
        aliases = {len(args): 0}
        args.append(earlier)
        specs.append(pl.BlockSpec(memory_space=pl.ANY))
    return pl.pallas_call(
        partial(mix_kernel, plan),
        out_shape=jax.ShapeDtypeStruct((2 * rows, cols), BF16),
        grid=(1,),
        in_specs=specs,
        out_specs=pl.BlockSpec((rows, cols), lambda i: (half, 0)),
        input_output_aliases=aliases,
        compiler_params=params(),
        cost_estimate=cost(2 * rows * depth * cols * len(plan), 2 * MIB),
        name="mix",
    )(*args)


def merge_kernel(span, radix, rows, end, decay, *refs):
    others, earlier, (state_ref, end_ref) = refs[: radix - 1], refs[radix - 1 : -2], refs[-2:]
    place = lax.axis_index("seq")
    mine = lax.rem(lax.div(place, span), radix)
    inner = rows * lax.rem(place, span)
    unit = rows * span
    rate = decay[...]

    def faded(count):
        return jnp.exp(-rate * jnp.full(rate.shape, count).astype(F32))

    state = earlier[0][...] if earlier else jnp.zeros(rate.shape, F32)
    total = faded(unit * (radix - 1 - mine)) * end[...]
    for step, other in enumerate(others, 1):
        theirs = lax.rem(mine + step, radix)
        value = other[...]
        ahead = jnp.full(rate.shape, mine - theirs) > 0
        state += jnp.where(ahead, faded(jnp.maximum(unit * (mine - theirs - 1), 0) + inner) * value, 0.0)
        total += faded(unit * (radix - 1 - theirs)) * value
    state_ref[...] = state
    end_ref[...] = total


def carry_in(end, decay, rows, work):
    devices = lax.axis_size("seq")
    shape = pltpu.VMEM(end.shape, F32)
    state, results, span = (), [], 1
    for radix in (2, 4, 4):
        others = []
        for step in range(1, radix):
            route = []
            for i in range(devices):
                inside = i // span % radix
                route.append((i + ((inside + step) % radix - inside) * span, i))
            others.append(near(lax.ppermute(end, "seq", route)))
        made = [work(len(results) + j, end) for j in range(2)] if span > 1 else []
        now, after = call(
            partial(merge_kernel, span, radix, rows),
            "merge",
            (shape, shape),
            (end, decay, *others, *state),
            16 * end.size,
            MIB,
        )
        if made and span * radix < devices:
            after, made = lax.optimization_barrier((after, made))
        results += made
        end, state = after, (now,)
        span *= radix
    return state[0], results


def call(kernel, name, out_shape, args, work, nbytes, scratch=()):
    specs = [vmem() for _ in args]
    return pl.pallas_call(
        kernel,
        out_shape=out_shape,
        in_specs=specs,
        out_specs=jax.tree.map(lambda _: vmem(), out_shape),
        scratch_shapes=list(scratch),
        compiler_params=params(),
        cost_estimate=cost(work, nbytes),
        name=name,
    )(*args)


def shards(tokens, w_in, short_filter, decay, residue, skip, w_out):
    rows = tokens.shape[0]
    channels = skip.shape[0]
    modes = decay.shape[0]
    half = rows // 2
    tiles = channels // LANES
    weights = near(jnp.transpose(w_in, (1, 0, 2)))
    streams, depth, _ = weights.shape
    taps, decay, residue = near(short_filter), near(decay), near(residue)
    skip = near(skip.reshape(1, channels))
    full = 2 * half * depth * streams * channels
    sums = (streams, half, channels)

    def own(low, high):
        return call(
            own_kernel,
            "own",
            (pltpu.VMEM(sums, F32), pltpu.VMEM(sums, F32)),
            (near(low), near(high), weights),
            full // 2,
            8 * MIB,
        )

    low_tok, high_tok, (low_own, high_own) = ring(tokens[:half], tokens[half:], own)
    low_tok, high_tok = [near(b) for b in low_tok], [near(b) for b in high_tok]
    high = call(
        high_kernel,
        "high",
        pltpu.VMEM(sums, BF16),
        (high_own, *high_tok[1:], weights),
        3 * full // 4,
        8 * MIB,
    )
    low_part = call(
        near_kernel,
        "near",
        pltpu.VMEM(sums, F32),
        (low_own, *low_tok[1:3], weights),
        full // 2,
        8 * MIB,
    )
    count = lax.axis_size("seq")
    halo = near(
        lax.ppermute(high[:, half - 16 :], "seq", [(i, i + 1) for i in range(count - 1)])
    )
    state_shape = pltpu.VMEM((modes, channels), F32)
    sub_shape = pltpu.VMEM((modes, SUB, channels), F32)
    high_sig, high_sub, late_end = call(
        late_kernel,
        "late",
        (pltpu.VMEM((tiles, half, LANES), F32), sub_shape, state_shape),
        (high, taps, decay),
        2 * half * channels * modes,
        3 * MIB,
        [pltpu.VMEM((2, half + SUB, channels), F32)],
    )
    low_sig, low_sub, mid, end = call(
        early_kernel,
        "early",
        (pltpu.VMEM((tiles, half + SUB, LANES), F32), sub_shape, state_shape, state_shape),
        (low_part, low_tok[3], weights, high, halo, taps, decay, late_end),
        full // 4,
        6 * MIB,
        [pltpu.VMEM((2, half + 2 * SUB, channels), F32)],
    )

    def work(tile, gate):
        sig, _ = lax.optimization_barrier((low_sig, gate))
        return call(
            partial(local_kernel, tile),
            "local",
            (pltpu.VMEM((rows, LANES), F32), pltpu.VMEM((rows, LANES), F32)),
            (
                low_part,
                low_tok[3],
                weights,
                high,
                halo,
                taps,
                decay,
                residue,
                skip,
                sig,
                low_sub,
                mid,
                high_sig,
                high_sub,
            ),
            8 * rows * channels * modes,
            4 * MIB,
            [pltpu.VMEM((1, rows + SUB, LANES), F32)],
        )

    state, local = carry_in(end, decay, rows, work)
    gates = [
        call(
            partial(gate_kernel, base),
            "gate",
            pltpu.VMEM((half, channels), BF16),
            (*[q for q, _ in local], *[p for _, p in local], state, decay, residue),
            half * channels * modes,
            2 * MIB,
        )
        for base in (0, half)
    ]
    low_gate, high_gate, _ = ring(*gates)
    w_out = near(w_out)
    out = mix_out(w_out, low_gate, (0, 3, 1, 2), 0, None, None)
    total = mix(w_out, high_gate[:3], (0, 3, 1))
    return mix_out(w_out, high_gate[3:], (2,), 1, total, out)


def solution(mesh):
    in_specs = (
        P("seq", "ch"),
        P(None, None, "ch"),
        P(None, None, "ch"),
        P(None, "ch"),
        P(None, "ch"),
        P("ch"),
        P(None, "ch"),
    )
    return jax.shard_map(
        shards, mesh=mesh, in_specs=in_specs, out_specs=P("seq", "ch"), check_vma=False
    )
```

```python
from functools import partial

import jax
import jax.numpy as jnp
from jax import lax
from jax.experimental import pallas as pl
from jax.experimental.pallas import tpu as pltpu
from jax.sharding import PartitionSpec as P

LANES = 128
SUB = 8
F32 = jnp.float32
BF16 = jnp.bfloat16
MIB = 1 << 20


def vmem():
    return pl.BlockSpec(memory_space=pltpu.VMEM)


def near(x):
    return pltpu.with_memory_space_constraint(x, pltpu.VMEM)


def params(mib=24):
    return pltpu.CompilerParams(vmem_limit_bytes=mib * MIB)


def cost(flops, nbytes, exps=0):
    return pl.CostEstimate(flops=flops, bytes_accessed=nbytes, transcendentals=exps)


def swap(block, flip):
    return lax.ppermute(block, "ch", [(i, i ^ flip) for i in range(lax.axis_size("ch"))])


def gather(low, high, work):
    low_three, high_one = swap(low, 3), swap(high, 1)
    done, low, high = lax.optimization_barrier((work(low, high), low, high))
    high_three, low_one = swap(high, 3), swap(low, 1)
    low_two, high_two = swap(low_three, 1), swap(high_one, 3)
    return (low, low_three, low_one, low_two), (high, high_three, high_one, high_two), done


def source(step, depth):
    owner = lax.bitwise_xor(lax.axis_index("ch"), step)
    return pl.ds(pl.multiple_of(owner * depth, depth), depth)


def own_kernel(block, w_ref, out_ref):
    depth = block.shape[1]
    for stream in range(w_ref.shape[0]):
        part = w_ref[stream, source(0, depth), :]
        out_ref[stream] = jnp.dot(block[...], part, preferred_element_type=F32)


def near_kernel(low_part, high_part, low_left, low_right, high_left, high_right, w_ref, low_ref, high_ref):
    depth = low_left.shape[1]
    for stream in range(w_ref.shape[0]):
        left = w_ref[stream, source(3, depth), :]
        right = w_ref[stream, source(1, depth), :]
        low_ref[stream] = (
            low_part[stream]
            + jnp.dot(low_left[...], left, preferred_element_type=F32)
            + jnp.dot(low_right[...], right, preferred_element_type=F32)
        )
        high_ref[stream] = (
            high_part[stream]
            + jnp.dot(high_left[...], left, preferred_element_type=F32)
            + jnp.dot(high_right[...], right, preferred_element_type=F32)
        )


def far_kernel(low_part, high_part, low_far, high_far, w_ref, out_ref):
    half, depth = low_far.shape
    for stream in range(w_ref.shape[0]):
        weights = w_ref[stream, source(2, depth), :]
        for base, part, far in ((0, low_part, low_far), (half, high_part, high_far)):
            total = part[stream] + jnp.dot(far[...], weights, preferred_element_type=F32)
            out_ref[stream, pl.ds(base, half), :] = total.astype(BF16)


def filtered(ext, slot, taps, stream, at, size, lanes, width):
    total = taps[stream, 0:1, lanes] * ext[slot, pl.ds(at + SUB, size), width]
    for lag in range(1, 3):
        total += taps[stream, lag : lag + 1, lanes] * ext[slot, pl.ds(at + SUB - lag, size), width]
    return total


def tile_of(tile):
    return slice(tile * LANES, (tile + 1) * LANES)


def spread(ref, row, lanes):
    return jnp.broadcast_to(ref[row : row + 1, lanes], (SUB, LANES))


def tree(terms):
    while len(terms) > 1:
        terms = [sum(terms[j : j + 2]) for j in range(0, len(terms), 2)]
    return terms[0]


def prepare_kernel(decay, residue, fade_ref, remain_ref, stride_ref, lead_ref, *, steps):
    rate = decay[...]
    fade_ref[...] = jnp.exp(-rate)
    stride_ref[...] = jnp.exp(-float(SUB) * rate)
    place = lax.broadcasted_iota(jnp.int32, (SUB, rate.shape[1]), 0)
    later = (SUB - 1 - place).astype(F32) * steps
    ahead = (1 + place).astype(F32)
    for m in range(rate.shape[0]):
        one = jnp.broadcast_to(decay[m : m + 1, :], place.shape)
        remain_ref[m] = jnp.exp(-one * later)
        lead_ref[m] = residue[m : m + 1, :] * jnp.sqrt(one) * jnp.exp(-one * ahead)


def early_kernel(proj, taps, fade_in, remain, sig, sub_ref, end_ref, ext):
    tiles, rows, _ = sig.shape
    modes = fade_in.shape[0]
    steps = rows // SUB
    for slot in range(2):
        ext[slot, 0:SUB, :] = jnp.zeros((SUB, ext.shape[2]), F32)
        for at in range(0, rows, 64):
            ext[slot, pl.ds(at + SUB, 64), :] = proj[slot + 1, pl.ds(at, 64), :].astype(F32)
    kept = lax.broadcasted_iota(jnp.int32, (64, LANES), 0) >= 2
    for tile in range(tiles):
        lanes = tile_of(tile)
        for at in range(0, rows, 64):
            value = filtered(ext, 0, taps, 1, at, 64, lanes, lanes)
            value *= filtered(ext, 1, taps, 2, at, 64, lanes, lanes)
            if at == 0:
                value = jnp.where(kept, value, 0.0)
            sig[tile, pl.ds(at, 64), :] = value
        fade = [spread(fade_in, m, lanes) for m in range(modes)]

        def step(i, held):
            now = sig[tile, pl.ds(i, SUB, stride=steps), :]
            return tuple(f * h + now for f, h in zip(fade, held))

        zero = tuple(jnp.zeros((SUB, LANES), F32) for _ in range(modes))
        held = lax.fori_loop(0, steps, step, zero, unroll=8)
        for m in range(modes):
            sub_ref[m, :, lanes] = held[m]
            end_ref[m : m + 1, lanes] = jnp.sum(
                held[m] * remain[m, :, lanes], axis=0, keepdims=True
            )


def preceding(halo, stream, lanes):
    value = halo[stream, 8:16, lanes].astype(F32)
    return jnp.where(jnp.full(value.shape, lax.axis_index("seq")) > 0, value, 0.0)


def edge_kernel(rows, proj, halo, taps, decay, end, edge_ref, out_ref):
    value = None
    for stream in (1, 2):
        first = proj[stream, 0:16, :].astype(F32)[0:SUB]
        joined = jnp.concatenate([preceding(halo, stream, slice(None)), first], 0)
        total = taps[stream, 0:1, :] * joined[SUB:]
        for lag in range(1, 3):
            total += taps[stream, lag : lag + 1, :] * joined[SUB - lag : 2 * SUB - lag]
        value = total if value is None else value * total
    edge_ref[...] = value
    rate = decay[...]
    out_ref[...] = (
        end[...]
        + jnp.exp(-float(rows - 1) * rate) * value[0:1]
        + jnp.exp(-float(rows - 2) * rate) * value[1:2]
    )


def local_kernel(
    tile, proj, halo, taps, decay, residue, skip, sig, sub, edge, query_ref, out_ref, ext
):
    lanes = tile_of(tile)
    whole = slice(0, LANES)
    modes = decay.shape[0]
    rows = sig.shape[1]
    steps = rows // SUB
    ext[0, 0:SUB, :] = preceding(halo, 0, lanes)
    for at in range(0, rows, 64):
        ext[0, pl.ds(at + SUB, 64), :] = proj[0, pl.ds(at, 64), lanes].astype(F32)
    for at in range(0, rows, 64):
        query_ref[pl.ds(at, 64), :] = filtered(ext, 0, taps, 0, at, 64, lanes, whole)

    place = lax.broadcasted_iota(jnp.int32, (SUB, LANES), 0)
    rates = [spread(decay, m, lanes) for m in range(modes)]
    fade = [jnp.exp(-r) for r in rates]
    gain = [residue[m : m + 1, lanes] * jnp.sqrt(r) for m, r in enumerate(rates)]
    direct = spread(skip, 0, lanes)
    one, two = edge[0:1, lanes], edge[1:2, lanes]
    start = []
    for m in range(modes):
        extra = jnp.exp(-rates[m] * float(steps - 1)) * one + jnp.exp(-rates[m] * float(steps - 2)) * two
        first = sub[m, :, lanes] + jnp.where(place == 0, extra, 0.0)
        run = jnp.where(place >= 1, pltpu.roll(first, 1, 0), 0.0)
        for shift in (1, 2, 4):
            before = jnp.where(place >= shift, pltpu.roll(run, shift, 0), 0.0)
            run = run + jnp.exp(-rates[m] * float(steps * shift)) * before
        start.append(run)

    def advance(i, held, more=None):
        at = pl.ds(i, SUB, stride=steps)
        now = sig[tile, at, :]
        if more is not None:
            now += jnp.where(place == 0, more, 0.0)
        held = tuple(f * h + now for f, h in zip(fade, held))
        out_ref[at, :] = tree([g * h for g, h in zip(gain, held)] + [direct * now])
        return held

    held = advance(1, advance(0, tuple(start), one), two)
    lax.fori_loop(2, steps, advance, held, unroll=2)


def gate_kernel(*refs):
    tiles = 4
    query, part = refs[:tiles], refs[tiles : 2 * tiles]
    state, stride, lead, low_ref, high_ref = refs[2 * tiles :]
    modes = state.shape[0]
    rows = low_ref.shape[0]
    for tile in range(tiles):
        lanes = tile_of(tile)
        fade = [spread(stride, m, lanes) for m in range(modes)]
        first = tuple(lead[m, :, lanes] * spread(state, m, lanes) for m in range(modes))

        def piece(at, held):
            value = query[tile][pl.ds(at, SUB), :] * (
                part[tile][pl.ds(at, SUB), :] + tree(list(held))
            )
            return value, tuple(f * h for f, h in zip(fade, held))

        def step(base, out_ref, i, held):
            at = pl.multiple_of(i * 16, 16)
            one, held = piece(at + base, held)
            two, held = piece(at + base + SUB, held)
            out_ref[pl.ds(at, 16), lanes] = jnp.concatenate([one, two], 0).astype(BF16)
            return held

        held = lax.fori_loop(0, rows // 16, partial(step, 0, low_ref), first, unroll=4)
        lax.fori_loop(0, rows // 16, partial(step, rows, high_ref), held, unroll=4)


def mix_kernel(plan, w_ref, *refs):
    blocks, rest = refs[: len(plan)], refs[len(plan) :]
    out_ref = rest[-1]
    depth = blocks[0].shape[1]
    total = None if len(rest) == 1 else rest[0][...]
    for block, step in zip(blocks, plan):
        term = jnp.dot(block[...], w_ref[source(step, depth), :], preferred_element_type=F32)
        total = term if total is None else total + term
    out_ref[...] = total


def last_kernel(w_ref, low, high, low_part, high_part, out_ref):
    rows, depth = low.shape
    weights = w_ref[source(2, depth), :]
    for at, block, part in ((0, low, low_part), (rows, high, high_part)):
        total = part[...] + jnp.dot(block[...], weights, preferred_element_type=F32)
        out_ref[pl.ds(at, rows), :] = total.astype(BF16)


def merge_kernel(span, radix, rows, end, decay, *refs):
    others, rest = refs[: radix - 1], list(refs[radix - 1 :])
    earlier = [rest.pop(0)] if span > 1 else []
    state_ref = rest.pop(0)
    place = lax.axis_index("seq")
    mine = lax.rem(lax.div(place, span), radix)
    inner = rows * lax.rem(place, span)
    unit = rows * span
    rate = decay[...]

    def faded(count):
        return jnp.exp(-rate * jnp.full(rate.shape, count).astype(F32))

    state = earlier[0][...] if earlier else jnp.zeros(rate.shape, F32)
    total = faded(unit * (radix - 1 - mine)) * end[...]
    for step, other in enumerate(others, 1):
        theirs = lax.rem(mine + step, radix)
        value = other[...]
        ahead = jnp.full(rate.shape, mine - theirs) > 0
        state += jnp.where(ahead, faded(jnp.maximum(unit * (mine - theirs - 1), 0) + inner) * value, 0.0)
        total += faded(unit * (radix - 1 - theirs)) * value
    state_ref[...] = state
    if rest:
        rest[0][...] = total


def carry_in(end, decay, rows, work):
    devices = lax.axis_size("seq")
    shape = pltpu.VMEM(end.shape, F32)
    state, results, span = (), [], 1
    for radix in (2, 4, 4):
        others = []
        for step in range(1, radix):
            route = []
            for i in range(devices):
                inside = i // span % radix
                route.append((i + ((inside + step) % radix - inside) * span, i))
            others.append(near(lax.ppermute(end, "seq", route)))
        made = [work(len(results) + j, end) for j in range(2)] if span > 1 else []
        final = span * radix == devices
        now, *after = call(
            partial(merge_kernel, span, radix, rows),
            "merge",
            (shape,) if final else (shape, shape),
            (end, decay, *others, *state),
            16 * end.size,
            MIB,
        )
        if made and not final:
            after, made = lax.optimization_barrier((after, made))
        results += made
        end, state = after[0] if after else None, (now,)
        span *= radix
    return state[0], results


def call(kernel, name, out_shape, args, work, nbytes, scratch=()):
    specs = [vmem() for _ in args]
    return pl.pallas_call(
        kernel,
        out_shape=out_shape,
        in_specs=specs,
        out_specs=jax.tree.map(lambda _: vmem(), out_shape),
        scratch_shapes=list(scratch),
        compiler_params=params(),
        cost_estimate=cost(work, nbytes),
        name=name,
    )(*args)


def shards(tokens, w_in, short_filter, decay, residue, skip, w_out):
    rows = tokens.shape[0]
    channels = skip.shape[0]
    modes = decay.shape[0]
    half = rows // 2
    tiles = channels // LANES
    weights = near(jnp.transpose(w_in, (1, 0, 2)))
    streams, depth, _ = weights.shape
    taps, decay, residue = near(short_filter), near(decay), near(residue)
    skip = near(skip.reshape(1, channels))
    full = 2 * half * depth * streams * channels
    sums = pltpu.VMEM((streams, half, channels), F32)
    rates = pltpu.VMEM((modes, channels), F32)
    ranks = pltpu.VMEM((modes, SUB, channels), F32)
    fade, remain, stride, lead = call(
        partial(prepare_kernel, steps=rows // SUB),
        "prepare",
        (rates, ranks, rates, ranks),
        (decay, residue),
        16 * SUB * channels,
        MIB,
    )

    def own(block):
        return call(own_kernel, "own", sums, (near(block), weights), full // 4, 8 * MIB)

    low_tok, high_tok, low_own = gather(tokens[:half], tokens[half:], lambda low, high: own(low))
    high_own = own(high_tok[0])
    low_tok, high_tok = [near(b) for b in low_tok], [near(b) for b in high_tok]
    low_part, high_part = call(
        near_kernel,
        "near",
        (sums, sums),
        (low_own, high_own, *low_tok[1:3], *high_tok[1:3], weights),
        full,
        8 * MIB,
    )
    proj = call(
        far_kernel,
        "far",
        pltpu.VMEM((streams, rows, channels), BF16),
        (low_part, high_part, low_tok[3], high_tok[3], weights),
        full // 2,
        6 * MIB,
    )
    count = lax.axis_size("seq")
    tail = proj[:, rows - 16 :]
    halo = near(lax.ppermute(tail, "seq", [(i, (i + 1) % count) for i in range(count)]))
    proj, _ = lax.optimization_barrier((proj, tail))
    sig, sub, end = call(
        early_kernel,
        "early",
        (
            pltpu.VMEM((tiles, rows, LANES), F32),
            pltpu.VMEM((modes, SUB, channels), F32),
            pltpu.VMEM((modes, channels), F32),
        ),
        (proj, taps, fade, remain),
        full // 2,
        6 * MIB,
        [pltpu.VMEM((2, rows + SUB, channels), F32)],
    )
    edge, end = call(
        partial(edge_kernel, rows),
        "edge",
        (pltpu.VMEM((SUB, channels), F32), pltpu.VMEM((modes, channels), F32)),
        (proj, halo, taps, decay, end),
        modes * channels,
        MIB,
    )

    def work(tile, gate):
        own_sig, _ = lax.optimization_barrier((sig, gate))
        return call(
            partial(local_kernel, tile),
            "local",
            (pltpu.VMEM((rows, LANES), F32), pltpu.VMEM((rows, LANES), F32)),
            (proj, halo, taps, decay, residue, skip, own_sig, sub, edge),
            8 * rows * channels * modes,
            4 * MIB,
            [pltpu.VMEM((1, rows + SUB, LANES), F32)],
        )

    state, local = carry_in(end, decay, rows, work)
    gates = call(
        gate_kernel,
        "gate",
        (pltpu.VMEM((half, channels), BF16), pltpu.VMEM((half, channels), BF16)),
        (*[q for q, _ in local], *[p for _, p in local], state, stride, lead),
        rows * channels * modes,
        4 * MIB,
    )
    w_out = near(w_out)
    totals = pltpu.VMEM((half, w_out.shape[1]), F32)

    def mix(blocks, plan, *earlier):
        return call(
            partial(mix_kernel, plan),
            "mix",
            totals,
            (w_out, *[near(block) for block in blocks], *earlier),
            2 * half * channels * channels * len(plan),
            2 * MIB,
        )

    low_gate, high_gate, (low_sum, high_sum) = gather(
        *gates, lambda low, high: [mix([block], (0,)) for block in (low, high)]
    )
    return call(
        last_kernel,
        "last",
        jax.ShapeDtypeStruct((rows, w_out.shape[1]), BF16),
        (
            w_out,
            near(low_gate[3]),
            near(high_gate[3]),
            mix(low_gate[1:3], (3, 1), low_sum),
            mix(high_gate[1:3], (3, 1), high_sum),
        ),
        4 * half * channels * channels,
        2 * MIB,
    )


def solution(mesh):
    in_specs = (
        P("seq", "ch"),
        P(None, None, "ch"),
        P(None, None, "ch"),
        P(None, "ch"),
        P(None, "ch"),
        P("ch"),
        P(None, "ch"),
    )
    return jax.shard_map(
        shards, mesh=mesh, in_specs=in_specs, out_specs=P("seq", "ch"), check_vma=False
    )
```

```python
from functools import partial

import jax
import jax.numpy as jnp
from jax import lax
from jax.experimental import pallas as pl
from jax.experimental.pallas import tpu as pltpu
from jax.sharding import PartitionSpec as P

LANES = 128
SUB = 8
F32 = jnp.float32
BF16 = jnp.bfloat16
MIB = 1 << 20


def vmem():
    return pl.BlockSpec(memory_space=pltpu.VMEM)


def near(x):
    return pltpu.with_memory_space_constraint(x, pltpu.VMEM)


def params(mib=24):
    return pltpu.CompilerParams(vmem_limit_bytes=mib * MIB)


def cost(flops, nbytes, exps=0):
    return pl.CostEstimate(flops=flops, bytes_accessed=nbytes, transcendentals=exps)


def swap(block, flip):
    return lax.ppermute(block, "ch", [(i, i ^ flip) for i in range(lax.axis_size("ch"))])


def gather(low, high, work):
    low_three, high_one = swap(low, 3), swap(high, 1)
    done, low, high = lax.optimization_barrier((work(low, high), low, high))
    high_three, low_one = swap(high, 3), swap(low, 1)
    low_two, high_two = swap(low_three, 1), swap(high_one, 3)
    return (low, low_three, low_one, low_two), (high, high_three, high_one, high_two), done


def source(step, depth):
    owner = lax.bitwise_xor(lax.axis_index("ch"), step)
    return pl.ds(pl.multiple_of(owner * depth, depth), depth)


def own_kernel(block, w_ref, out_ref):
    depth = block.shape[1]
    for stream in range(w_ref.shape[0]):
        part = w_ref[stream, source(0, depth), :]
        out_ref[stream] = jnp.dot(block[...], part, preferred_element_type=F32)


def near_kernel(low_part, high_part, low_left, low_right, high_left, high_right, w_ref, low_ref, high_ref):
    depth = low_left.shape[1]
    for stream in range(w_ref.shape[0]):
        left = w_ref[stream, source(3, depth), :]
        right = w_ref[stream, source(1, depth), :]
        low_ref[stream] = (
            low_part[stream]
            + jnp.dot(low_left[...], left, preferred_element_type=F32)
            + jnp.dot(low_right[...], right, preferred_element_type=F32)
        )
        high_ref[stream] = (
            high_part[stream]
            + jnp.dot(high_left[...], left, preferred_element_type=F32)
            + jnp.dot(high_right[...], right, preferred_element_type=F32)
        )


def far_kernel(low_part, high_part, low_far, high_far, w_ref, out_ref):
    half, depth = low_far.shape
    for stream in range(w_ref.shape[0]):
        weights = w_ref[stream, source(2, depth), :]
        for base, part, far in ((0, low_part, low_far), (half, high_part, high_far)):
            total = part[stream] + jnp.dot(far[...], weights, preferred_element_type=F32)
            out_ref[stream, pl.ds(base, half), :] = total.astype(BF16)


def filtered(ext, slot, taps, stream, at, size, lanes, width):
    total = taps[stream, 0:1, lanes] * ext[slot, pl.ds(at + SUB, size), width]
    for lag in range(1, 3):
        total += taps[stream, lag : lag + 1, lanes] * ext[slot, pl.ds(at + SUB - lag, size), width]
    return total


def tile_of(tile):
    return slice(tile * LANES, (tile + 1) * LANES)


def spread(ref, row, lanes):
    return jnp.broadcast_to(ref[row : row + 1, lanes], (SUB, LANES))


def tree(terms):
    while len(terms) > 1:
        terms = [sum(terms[j : j + 2]) for j in range(0, len(terms), 2)]
    return terms[0]


def prepare_kernel(decay, residue, fade_ref, remain_ref, stride_ref, lead_ref, *, steps):
    rate = decay[...]
    fade_ref[...] = jnp.exp(-rate)
    stride_ref[...] = jnp.exp(-float(SUB) * rate)
    place = lax.broadcasted_iota(jnp.int32, (SUB, rate.shape[1]), 0)
    later = (SUB - 1 - place).astype(F32) * steps
    ahead = (1 + place).astype(F32)
    for m in range(rate.shape[0]):
        one = jnp.broadcast_to(decay[m : m + 1, :], place.shape)
        remain_ref[m] = jnp.exp(-one * later)
        lead_ref[m] = residue[m : m + 1, :] * jnp.sqrt(one) * jnp.exp(-one * ahead)


def early_kernel(proj, taps, fade_in, remain, sig, sub_ref, end_ref, ext):
    tiles, rows, _ = sig.shape
    modes = fade_in.shape[0]
    steps = rows // SUB
    for slot in range(2):
        ext[slot, 0:SUB, :] = jnp.zeros((SUB, ext.shape[2]), F32)
        for at in range(0, rows, 64):
            ext[slot, pl.ds(at + SUB, 64), :] = proj[slot + 1, pl.ds(at, 64), :].astype(F32)
    kept = lax.broadcasted_iota(jnp.int32, (64, LANES), 0) >= 2
    for tile in range(tiles):
        lanes = tile_of(tile)
        for at in range(0, rows, 64):
            value = filtered(ext, 0, taps, 1, at, 64, lanes, lanes)
            value *= filtered(ext, 1, taps, 2, at, 64, lanes, lanes)
            if at == 0:
                value = jnp.where(kept, value, 0.0)
            sig[tile, pl.ds(at, 64), :] = value
        fade = [spread(fade_in, m, lanes) for m in range(modes)]

        def step(i, held):
            now = sig[tile, pl.ds(i, SUB, stride=steps), :]
            return tuple(f * h + now for f, h in zip(fade, held))

        zero = tuple(jnp.zeros((SUB, LANES), F32) for _ in range(modes))
        held = lax.fori_loop(0, steps, step, zero, unroll=16)
        for m in range(modes):
            sub_ref[m, :, lanes] = held[m]
            end_ref[m : m + 1, lanes] = jnp.sum(
                held[m] * remain[m, :, lanes], axis=0, keepdims=True
            )


def preceding(halo, stream, lanes):
    value = halo[stream, 8:16, lanes].astype(F32)
    return jnp.where(jnp.full(value.shape, lax.axis_index("seq")) > 0, value, 0.0)


def edge_kernel(rows, proj, halo, taps, decay, end, edge_ref, out_ref):
    value = None
    for stream in (1, 2):
        first = proj[stream, 0:16, :].astype(F32)[0:SUB]
        joined = jnp.concatenate([preceding(halo, stream, slice(None)), first], 0)
        total = taps[stream, 0:1, :] * joined[SUB:]
        for lag in range(1, 3):
            total += taps[stream, lag : lag + 1, :] * joined[SUB - lag : 2 * SUB - lag]
        value = total if value is None else value * total
    edge_ref[...] = value
    rate = decay[...]
    out_ref[...] = (
        end[...]
        + jnp.exp(-float(rows - 1) * rate) * value[0:1]
        + jnp.exp(-float(rows - 2) * rate) * value[1:2]
    )


def local_kernel(
    tile, proj, halo, taps, decay, residue, skip, sig, sub, edge, query_ref, out_ref, ext
):
    lanes = tile_of(tile)
    whole = slice(0, LANES)
    modes = decay.shape[0]
    rows = sig.shape[1]
    steps = rows // SUB
    ext[0, 0:SUB, :] = preceding(halo, 0, lanes)
    for at in range(0, rows, 64):
        ext[0, pl.ds(at + SUB, 64), :] = proj[0, pl.ds(at, 64), lanes].astype(F32)
    for at in range(0, rows, 64):
        query_ref[pl.ds(at, 64), :] = filtered(ext, 0, taps, 0, at, 64, lanes, whole)

    place = lax.broadcasted_iota(jnp.int32, (SUB, LANES), 0)
    rates = [spread(decay, m, lanes) for m in range(modes)]
    fade = [jnp.exp(-r) for r in rates]
    gain = [residue[m : m + 1, lanes] * jnp.sqrt(r) for m, r in enumerate(rates)]
    direct = spread(skip, 0, lanes)
    one, two = edge[0:1, lanes], edge[1:2, lanes]
    start = []
    for m in range(modes):
        extra = jnp.exp(-rates[m] * float(steps - 1)) * one + jnp.exp(-rates[m] * float(steps - 2)) * two
        first = sub[m, :, lanes] + jnp.where(place == 0, extra, 0.0)
        run = jnp.where(place >= 1, pltpu.roll(first, 1, 0), 0.0)
        for shift in (1, 2, 4):
            before = jnp.where(place >= shift, pltpu.roll(run, shift, 0), 0.0)
            run = run + jnp.exp(-rates[m] * float(steps * shift)) * before
        start.append(run)

    def advance(i, held, more=None):
        at = pl.ds(i, SUB, stride=steps)
        now = sig[tile, at, :]
        if more is not None:
            now += jnp.where(place == 0, more, 0.0)
        held = tuple(f * h + now for f, h in zip(fade, held))
        out_ref[at, :] = tree([g * h for g, h in zip(gain, held)] + [direct * now])
        return held

    held = advance(1, advance(0, tuple(start), one), two)
    lax.fori_loop(2, steps, advance, held, unroll=2)


def gate_kernel(*refs):
    tiles = 4
    query, part = refs[:tiles], refs[tiles : 2 * tiles]
    state, stride, lead, low_ref, high_ref = refs[2 * tiles :]
    modes = state.shape[0]
    rows = low_ref.shape[0]
    for tile in range(tiles):
        lanes = tile_of(tile)
        fade = [spread(stride, m, lanes) for m in range(modes)]
        first = tuple(lead[m, :, lanes] * spread(state, m, lanes) for m in range(modes))

        def piece(at, held):
            value = query[tile][pl.ds(at, SUB), :] * (
                part[tile][pl.ds(at, SUB), :] + tree(list(held))
            )
            return value, tuple(f * h for f, h in zip(fade, held))

        def step(base, out_ref, i, held):
            at = pl.multiple_of(i * 16, 16)
            one, held = piece(at + base, held)
            two, held = piece(at + base + SUB, held)
            out_ref[pl.ds(at, 16), lanes] = jnp.concatenate([one, two], 0).astype(BF16)
            return held

        held = lax.fori_loop(0, rows // 16, partial(step, 0, low_ref), first, unroll=8)
        lax.fori_loop(0, rows // 16, partial(step, rows, high_ref), held, unroll=8)


def mix_kernel(plan, w_ref, *refs):
    blocks, rest = refs[: len(plan)], refs[len(plan) :]
    out_ref = rest[-1]
    depth = blocks[0].shape[1]
    total = None if len(rest) == 1 else rest[0][...]
    for block, step in zip(blocks, plan):
        term = jnp.dot(block[...], w_ref[source(step, depth), :], preferred_element_type=F32)
        total = term if total is None else total + term
    out_ref[...] = total


def last_kernel(w_ref, low, high, low_part, high_part, out_ref):
    rows, depth = low.shape
    weights = w_ref[source(2, depth), :]
    for at, block, part in ((0, low, low_part), (rows, high, high_part)):
        total = part[...] + jnp.dot(block[...], weights, preferred_element_type=F32)
        out_ref[pl.ds(at, rows), :] = total.astype(BF16)


def merge_kernel(span, radix, rows, end, decay, *refs):
    others, rest = refs[: radix - 1], list(refs[radix - 1 :])
    earlier = [rest.pop(0)] if span > 1 else []
    state_ref = rest.pop(0)
    place = lax.axis_index("seq")
    mine = lax.rem(lax.div(place, span), radix)
    inner = rows * lax.rem(place, span)
    unit = rows * span
    rate = decay[...]

    def faded(count):
        return jnp.exp(-rate * jnp.full(rate.shape, count).astype(F32))

    state = earlier[0][...] if earlier else jnp.zeros(rate.shape, F32)
    total = faded(unit * (radix - 1 - mine)) * end[...]
    for step, other in enumerate(others, 1):
        theirs = lax.rem(mine + step, radix)
        value = other[...]
        ahead = jnp.full(rate.shape, mine - theirs) > 0
        state += jnp.where(ahead, faded(jnp.maximum(unit * (mine - theirs - 1), 0) + inner) * value, 0.0)
        total += faded(unit * (radix - 1 - theirs)) * value
    state_ref[...] = state
    if rest:
        rest[0][...] = total


def carry_in(end, decay, rows, work):
    devices = lax.axis_size("seq")
    shape = pltpu.VMEM(end.shape, F32)
    state, results, span = (), [], 1
    for radix in (2, 4, 4):
        others = []
        for step in range(1, radix):
            route = []
            for i in range(devices):
                inside = i // span % radix
                route.append((i + ((inside + step) % radix - inside) * span, i))
            others.append(near(lax.ppermute(end, "seq", route)))
        made = [work(len(results) + j, end) for j in range(2)] if span > 1 else []
        final = span * radix == devices
        now, *after = call(
            partial(merge_kernel, span, radix, rows),
            "merge",
            (shape,) if final else (shape, shape),
            (end, decay, *others, *state),
            16 * end.size,
            MIB,
        )
        if made and not final:
            after, made = lax.optimization_barrier((after, made))
        results += made
        end, state = after[0] if after else None, (now,)
        span *= radix
    return state[0], results


def call(kernel, name, out_shape, args, work, nbytes, scratch=()):
    specs = [vmem() for _ in args]
    return pl.pallas_call(
        kernel,
        out_shape=out_shape,
        in_specs=specs,
        out_specs=jax.tree.map(lambda _: vmem(), out_shape),
        scratch_shapes=list(scratch),
        compiler_params=params(),
        cost_estimate=cost(work, nbytes),
        name=name,
    )(*args)


def shards(tokens, w_in, short_filter, decay, residue, skip, w_out):
    rows = tokens.shape[0]
    channels = skip.shape[0]
    modes = decay.shape[0]
    half = rows // 2
    tiles = channels // LANES
    weights = near(jnp.transpose(w_in, (1, 0, 2)))
    streams, depth, _ = weights.shape
    taps, decay, residue = near(short_filter), near(decay), near(residue)
    skip = near(skip.reshape(1, channels))
    full = 2 * half * depth * streams * channels
    sums = pltpu.VMEM((streams, half, channels), F32)
    rates = pltpu.VMEM((modes, channels), F32)
    ranks = pltpu.VMEM((modes, SUB, channels), F32)
    fade, remain, stride, lead = call(
        partial(prepare_kernel, steps=rows // SUB),
        "prepare",
        (rates, ranks, rates, ranks),
        (decay, residue),
        16 * SUB * channels,
        MIB,
    )

    def own(block):
        return call(own_kernel, "own", sums, (near(block), weights), full // 4, 8 * MIB)

    low_tok, high_tok, low_own = gather(tokens[:half], tokens[half:], lambda low, high: own(low))
    high_own = own(high_tok[0])
    low_tok, high_tok = [near(b) for b in low_tok], [near(b) for b in high_tok]
    low_part, high_part = call(
        near_kernel,
        "near",
        (sums, sums),
        (low_own, high_own, *low_tok[1:3], *high_tok[1:3], weights),
        full,
        8 * MIB,
    )
    proj = call(
        far_kernel,
        "far",
        pltpu.VMEM((streams, rows, channels), BF16),
        (low_part, high_part, low_tok[3], high_tok[3], weights),
        full // 2,
        6 * MIB,
    )
    count = lax.axis_size("seq")
    tail = proj[:, rows - 16 :]
    halo = near(lax.ppermute(tail, "seq", [(i, (i + 1) % count) for i in range(count)]))
    proj, _ = lax.optimization_barrier((proj, tail))
    sig, sub, end = call(
        early_kernel,
        "early",
        (
            pltpu.VMEM((tiles, rows, LANES), F32),
            pltpu.VMEM((modes, SUB, channels), F32),
            pltpu.VMEM((modes, channels), F32),
        ),
        (proj, taps, fade, remain),
        full // 2,
        6 * MIB,
        [pltpu.VMEM((2, rows + SUB, channels), F32)],
    )
    edge, end = call(
        partial(edge_kernel, rows),
        "edge",
        (pltpu.VMEM((SUB, channels), F32), pltpu.VMEM((modes, channels), F32)),
        (proj, halo, taps, decay, end),
        modes * channels,
        MIB,
    )

    def work(tile, gate):
        own_sig, _ = lax.optimization_barrier((sig, gate))
        return call(
            partial(local_kernel, tile),
            "local",
            (pltpu.VMEM((rows, LANES), F32), pltpu.VMEM((rows, LANES), F32)),
            (proj, halo, taps, decay, residue, skip, own_sig, sub, edge),
            8 * rows * channels * modes,
            4 * MIB,
            [pltpu.VMEM((1, rows + SUB, LANES), F32)],
        )

    state, local = carry_in(end, decay, rows, work)
    gates = call(
        gate_kernel,
        "gate",
        (pltpu.VMEM((half, channels), BF16), pltpu.VMEM((half, channels), BF16)),
        (*[q for q, _ in local], *[p for _, p in local], state, stride, lead),
        rows * channels * modes,
        4 * MIB,
    )
    w_out = near(w_out)
    totals = pltpu.VMEM((half, w_out.shape[1]), F32)

    def mix(blocks, plan, *earlier):
        return call(
            partial(mix_kernel, plan),
            "mix",
            totals,
            (w_out, *[near(block) for block in blocks], *earlier),
            2 * half * channels * channels * len(plan),
            2 * MIB,
        )

    low_gate, high_gate, (low_sum, high_sum) = gather(
        *gates, lambda low, high: [mix([block], (0,)) for block in (low, high)]
    )
    return call(
        last_kernel,
        "last",
        jax.ShapeDtypeStruct((rows, w_out.shape[1]), BF16),
        (
            w_out,
            near(low_gate[3]),
            near(high_gate[3]),
            mix(low_gate[1:3], (3, 1), low_sum),
            mix(high_gate[1:3], (3, 1), high_sum),
        ),
        4 * half * channels * channels,
        2 * MIB,
    )


def solution(mesh):
    in_specs = (
        P("seq", "ch"),
        P(None, None, "ch"),
        P(None, None, "ch"),
        P(None, "ch"),
        P(None, "ch"),
        P("ch"),
        P(None, "ch"),
    )
    return jax.shard_map(
        shards, mesh=mesh, in_specs=in_specs, out_specs=P("seq", "ch"), check_vma=False
    )
```
